32 devices in a mesh: fsdp: 8 (over z, y), ctx: 4 (over x, core).
Axes of the slice: x: 2, y: 2, z: 4, core: 2. Of those that a mesh axis runs over, the one named last changes fastest.
Arguments:
- tokens: bfloat16 [16, 2048, 576], P('fsdp', 'ctx'), may hold values from -6 to 6
- cotangent: bfloat16 [16, 2048, 576], P('fsdp', 'ctx'), may hold values from -6 to 6
- span_order: int32 [8], replicated, may hold values from 0 to 7, each once
- norm_one: bfloat16 [576], P('fsdp'), may hold values from 0.5 to 1.5
- w_query: bfloat16 [576, 576], P('fsdp'), may hold values from -0.25 to 0.25
- w_key: bfloat16 [576, 192], P('fsdp'), may hold values from -0.25 to 0.25
- w_value: bfloat16 [576, 192], P('fsdp'), may hold values from -0.25 to 0.25
- w_out: bfloat16 [576, 576], P('fsdp'), may hold values from -1.5 to 1.5
- norm_two: bfloat16 [576], P('fsdp'), may hold values from 0.5 to 1.5
- w_gate: bfloat16 [576, 1536], P('fsdp'), may hold values from -0.25 to 0.25
- w_up: bfloat16 [576, 1536], P('fsdp'), may hold values from -0.25 to 0.25
- w_down: bfloat16 [1536, 576], P('fsdp'), may hold values from -0.15625 to 0.15625
Outputs:
- output: bfloat16 [16, 2048, 576], P('fsdp', 'ctx')
- grad_input: float32 [16, 2048, 576], P('fsdp', 'ctx')
- grad_norm_one: float32 [576], P('fsdp')
- grad_w_query: float32 [576, 576], P('fsdp')
- grad_w_key: float32 [576, 192], P('fsdp')
- grad_w_value: float32 [576, 192], P('fsdp')
- grad_w_out: float32 [576, 576], P('fsdp')
- grad_norm_two: float32 [576], P('fsdp')
- grad_w_gate: float32 [576, 1536], P('fsdp')
- grad_w_up: float32 [576, 1536], P('fsdp')
- grad_w_down: float32 [1536, 576], P('fsdp')
The draws below stay inside these ranges and needn't reach their ends.
Inputs may be any that keep to these rules, and one draw needn't show every extreme that they name: `span_order`: every span number appears once.
All inputs are finite; a program needn't handle non-finite values.
Results may differ from the reference program's by a relative error of at most 0.015.
Values may be sent and summed in bfloat16 or wider, within the bound.
A program may use at most 384 MiB of HBM per device.

```python
import jax
import jax.numpy as jnp
from jax import lax

D = 576
FF = 1536
Q_HEADS = 9
KV_HEADS = 3
HEAD = 64
SEQ_LEN = 2048
SEQS = 16
HQ = 576
KVW = 192
NCHUNK = 8
N_CTX = 4


def strengthened(array, stream_key, source, target, shards_of, factor):
    owner, partner = [(jnp.arange(array.shape[axis_at]) // (array.shape[axis_at] // shards_of)).reshape([-1 if axis == axis_at else 1 for axis in range(array.ndim)]) for axis_at in (source, target)]
    chosen = jax.random.permutation(stream_key, shards_of)[partner]
    strong = (owner == chosen) | (owner == (partner + shards_of // 2) % shards_of)
    return jnp.where(strong, factor * array, array)


def block_scale(stream_key, extent, cuts, least, top_value):
    def one(position, blocks):
        draws = jax.random.uniform(jax.random.fold_in(jax.random.fold_in(stream_key, 6), position), (blocks,), jnp.float32, least / len(cuts), top_value / len(cuts))
        return jnp.repeat(jnp.exp(draws), extent[position] // blocks).reshape((-1,) + (1,) * (len(extent) - position - 1))

    level = one(*cuts[0])
    for cut in cuts[1:]:
        level = level * one(*cut)
    return level


def scatter_about(stream_key, extent, width, limit, cuts=(), kind=jnp.bfloat16):
    result = width * jax.random.normal(stream_key, extent, jnp.float32)
    if cuts:
        result = result * block_scale(stream_key, extent, cuts, -0.22, 0.18)
    return jnp.clip(result, -limit, limit).astype(kind)


def bell_draw_with(stream_key, extent, spread, limit, shards, heavy, held_as=jnp.bfloat16):
    array = spread * jax.random.normal(stream_key, extent, jnp.float32)
    if shards:
        array = array * block_scale(stream_key, extent, shards, -0.22, 0.18)
    return jnp.clip(strengthened(array, jax.random.fold_in(stream_key, 3), *heavy), -limit, limit).astype(held_as)


def setup_inputs(seed: int = 0) -> dict:
    key_of = jax.random.split(jax.random.key(seed), 13)
    tokens = bell_draw_with(key_of[0], (SEQS, SEQ_LEN, D), 1.0, 6.0, ((0, 8), (1, 4)), (0, 2, 8, 2.0))
    cotangent = scatter_about(key_of[1], (SEQS, SEQ_LEN, D), 1.0, 6.0, ((0, 8), (1, 4)))
    span_order = jax.random.permutation(key_of[2], NCHUNK).astype(jnp.int32)
    norm_one = jnp.clip(1.0 + 0.1 * jax.random.normal(key_of[3], (D,), jnp.float32), 0.5, 1.5).astype(jnp.bfloat16)
    w_query = scatter_about(key_of[4], (D, HQ), D ** -0.5, 0.25, ((0, 8),))
    w_key = scatter_about(key_of[5], (D, KVW), D ** -0.5, 0.25, ((0, 8),))
    w_value = scatter_about(key_of[6], (D, KVW), D ** -0.5, 0.25, ((0, 8),))
    w_out = scatter_about(key_of[7], (HQ, D), 16 ** -0.5, 1.5, ((0, 8),))
    norm_two = jnp.clip(1.0 + 0.1 * jax.random.normal(key_of[8], (D,), jnp.float32), 0.5, 1.5).astype(jnp.bfloat16)
    w_gate = scatter_about(key_of[9], (D, FF), D ** -0.5, 0.25, ((0, 8),))
    w_up = scatter_about(key_of[10], (D, FF), D ** -0.5, 0.25, ((0, 8),))
    w_down = scatter_about(key_of[11], (FF, D), FF ** -0.5, 0.15625, ((0, 8),))
    return {"tokens": tokens, "cotangent": cotangent, "span_order": span_order, "norm_one": norm_one, "w_query": w_query, "w_key": w_key, "w_value": w_value, "w_out": w_out, "norm_two": norm_two, "w_gate": w_gate, "w_up": w_up, "w_down": w_down}


@jax.custom_vjp
def low(v):
    return lax.optimization_barrier(v.astype(jnp.bfloat16)).astype(jnp.float32)

@jax.custom_vjp
def low_back(v):
    return v

def low_keep(v):
    return (low(v), None)

def low_pass(kept, grad):
    return (grad,)

def back_keep(v):
    return (v, None)

def back_low(kept, grad):
    return (low(grad),)
low.defvjp(low_keep, low_pass)
low_back.defvjp(back_keep, back_low)
epsilon = 1e-05
rope_base = 100000.0
highest = lax.Precision.HIGHEST

def matmul(left_side, right_side):
    return jnp.dot(left_side, right_side, precision=highest, preferred_element_type=jnp.float32)

def rms_norm(values, gain_vector):
    scaling = lax.rsqrt(lax.optimization_barrier(jnp.mean(values * values, axis=-1, keepdims=True)) + epsilon)
    return values * scaling * gain_vector

def rotate(heads_in, positions):
    half_size = heads_in.shape[-1] // 2
    frequency = rope_base ** (-2.0 * jnp.arange(half_size, dtype=jnp.float32) / heads_in.shape[-1])
    angles = positions.astype(jnp.float32)[:, None] * frequency[None, :]
    cosine = jnp.cos(angles)[:, None, :]
    sine_part = jnp.sin(angles)[:, None, :]
    first_half = heads_in[..., :half_size]
    second_half = heads_in[..., half_size:]
    return jnp.concatenate([first_half * cosine - second_half * sine_part, second_half * cosine + first_half * sine_part], axis=-1)

def layer_forward(hidden_in, positions, norm_one, w_query, w_key, w_value, w_out, norm_two, w_gate, w_up, w_down):
    length = hidden_in.shape[0]
    group_size = Q_HEADS // KV_HEADS
    normed = low(rms_norm(hidden_in, norm_one))
    queries = low_back(matmul(normed, w_query)).reshape(length, Q_HEADS, HEAD)
    queries = low(rotate(queries, positions) * 0.125)
    keys_all = low_back(matmul(normed, w_key)).reshape(length, KV_HEADS, HEAD)
    keys_all = low(rotate(keys_all, positions))
    values_all = low(low_back(matmul(normed, w_value))).reshape(length, KV_HEADS, HEAD)
    block_rows = 512 if length % 512 == 0 else length
    grouped = queries.reshape(length // block_rows, block_rows, KV_HEADS, group_size, HEAD)
    query_places = positions.reshape(length // block_rows, block_rows)

    def attend(block_pair):
        block_query, block_places = block_pair
        scores = jnp.einsum('qkgd,skd->kgqs', block_query, keys_all, precision=highest)
        scores = low_back(scores)
        allowed = block_places[:, None] >= positions[None, :]
        scores = jnp.where(allowed[None, None], scores, -1e+30)
        weights = low(jax.nn.softmax(scores, axis=-1))
        return jnp.einsum('kgqs,skd->qkgd', weights, values_all, precision=highest)
    mixed_heads = lax.map(jax.checkpoint(attend), (grouped, query_places))
    attended = low(low_back(mixed_heads.reshape(length, Q_HEADS * HEAD)))
    branch = low_back(matmul(attended, w_out))
    middle = hidden_in + branch
    normed_two = low(rms_norm(middle, norm_two))
    gate_pre = low_back(matmul(normed_two, w_gate))
    up_pre = low_back(matmul(normed_two, w_up))
    inner_act = low(jax.nn.silu(gate_pre) * up_pre)
    return middle + low_back(matmul(inner_act, w_down))

def reference(tokens, cotangent, span_order, norm_one, w_query, w_key, w_value, w_out, norm_two, w_gate, w_up, w_down):
    span_size = SEQ_LEN // (2 * N_CTX)
    positions = (span_order[:, None] * span_size + jnp.arange(span_size, dtype=jnp.int32)[None, :]).reshape(SEQ_LEN)
    params = tuple((weight.astype(jnp.float32) for weight in (norm_one, w_query, w_key, w_value, w_out, norm_two, w_gate, w_up, w_down)))

    def forward(hidden_in, *weights):
        return layer_forward(hidden_in, positions, *weights)

    def one_sequence(running, inputs_pair):
        sequence, upstream = inputs_pair
        output, pullback = jax.vjp(forward, sequence.astype(jnp.float32), *params)
        gradients = pullback(upstream.astype(jnp.float32))
        summed = tuple((total_now + gradient for total_now, gradient in zip(running, gradients[1:])))
        return (summed, (output.astype(jnp.bfloat16), gradients[0]))
    initial = tuple((jnp.zeros_like(weight) for weight in params))
    totals, (outputs, input_grads) = lax.scan(one_sequence, initial, (tokens, cotangent))
    return (outputs, input_grads, totals[0], totals[1], totals[2], totals[3], totals[4], totals[5], totals[6], totals[7], totals[8])
```

```python
import functools

import jax
import jax.numpy as jnp
from jax import lax
from jax.experimental import pallas as pl
from jax.experimental.pallas import tpu as pltpu
from jax.sharding import PartitionSpec as P

Q_HEADS = 9
KV_HEADS = 3
HEAD = 64
GROUP = Q_HEADS // KV_HEADS
PAD = 128

epsilon = 1e-05
rope_base = 100000.0


def rms_norm(values, gain_vector):
    scaling = lax.rsqrt(jnp.mean(values * values, axis=-1, keepdims=True) + epsilon)
    return values * scaling * gain_vector


def rope_tables(positions):
    half_size = HEAD // 2
    frequency = rope_base ** (-2.0 * jnp.arange(half_size, dtype=jnp.float32) / HEAD)
    angles = frequency[:, None] * positions.astype(jnp.float32)[None, :]
    return jnp.cos(angles), jnp.sin(angles)


def rotate(features, cosine, sine_part):
    count = features.shape[1]
    pairs = features.reshape(-1, 2, HEAD // 2, count)
    first, second = pairs[:, 0], pairs[:, 1]
    turned = jnp.stack(
        [first * cosine - second * sine_part, second * cosine + first * sine_part], axis=1
    )
    return turned.reshape(features.shape)


def product(left_side, right_side, pattern):
    return jnp.einsum(pattern, left_side, right_side, preferred_element_type=jnp.float32)


def swish_gate(gate_in, upper_in):
    return jax.nn.silu(gate_in) * upper_in


def mm(left_side, right_side):
    return jnp.dot(left_side, right_side, preferred_element_type=jnp.float32)


def mm_nt(left_side, right_side):
    return lax.dot_general(
        left_side, right_side, (((1,), (1,)), ((), ())), preferred_element_type=jnp.float32
    )


def causal(span):
    shape = (span, GROUP * span)
    key_at = lax.broadcasted_iota(jnp.int32, shape, 0)
    query_at = lax.rem(lax.broadcasted_iota(jnp.int32, shape, 1), span)
    return key_at <= query_at


def heads_side_by_side(ref, part, span):
    columns = slice(part * span, (part + 1) * span)
    return jnp.concatenate(
        [ref[g * HEAD : (g + 1) * HEAD, columns] for g in range(GROUP)], axis=1
    )


def forward_kernel(span, holder_ref, place_ref, q_ref, kv_ref, o_ref, lse_ref, keys, values):
    spans = keys.shape[0]
    for c in range(spans // 2):
        for half in range(2):
            columns = slice(half * span, (half + 1) * span)
            keys[2 * c + half] = kv_ref[c, 0, :, columns].T
            values[2 * c + half] = kv_ref[c, 1, :, columns]
    for part in range(2):
        query = heads_side_by_side(q_ref, part, span)
        place = place_ref[part]
        own = holder_ref[place]
        scores = jnp.where(causal(span), mm(keys[own], query), -1e30)
        top = jnp.max(scores, axis=0, keepdims=True)
        raised = jnp.exp(scores - top)
        total = jnp.sum(raised, axis=0, keepdims=True)
        mixed = mm(values[own], raised.astype(jnp.bfloat16))

        def earlier(j, carry, query=query):
            top, total, mixed = carry
            held = holder_ref[j]
            scores = mm(keys[held], query)
            new_top = jnp.maximum(top, jnp.max(scores, axis=0, keepdims=True))
            shrink = jnp.exp(top - new_top)
            raised = jnp.exp(scores - new_top)
            total = total * shrink + jnp.sum(raised, axis=0, keepdims=True)
            mixed = mixed * shrink + mm(values[held], raised.astype(jnp.bfloat16))
            return new_top, total, mixed

        top, total, mixed = lax.fori_loop(0, place, earlier, (top, total, mixed))
        mixed = mixed / total
        lse = top + jnp.log(total)
        for g in range(GROUP):
            source = slice(g * span, (g + 1) * span)
            columns = slice(part * span, (part + 1) * span)
            o_ref[g * HEAD : (g + 1) * HEAD, columns] = mixed[:, source].astype(jnp.bfloat16)
            lse_ref[0, g : g + 1, columns] = lse[:, source]


def backward_kernel(
    span, holder_ref, place_ref, q_ref, do_ref, o_ref, lse_ref, kv_ref,
    dq_ref, dkv_ref, keys, keys_t, values, key_sum, value_sum, query_sum,
):
    spans = keys.shape[0]
    for c in range(spans // 2):
        for half in range(2):
            columns = slice(half * span, (half + 1) * span)
            keys[2 * c + half] = kv_ref[c, 0, :, columns].T
            keys_t[2 * c + half] = kv_ref[c, 0, :, columns]
            values[2 * c + half] = kv_ref[c, 1, :, columns].T
    key_sum[...] = jnp.zeros_like(key_sum)
    value_sum[...] = jnp.zeros_like(value_sum)
    for part in range(2):
        query = heads_side_by_side(q_ref, part, span)
        upstream = heads_side_by_side(do_ref, part, span)
        mixed = heads_side_by_side(o_ref, part, span)
        columns = slice(part * span, (part + 1) * span)
        lse = jnp.concatenate([lse_ref[0, g : g + 1, columns] for g in range(GROUP)], axis=1)
        delta = jnp.sum(
            upstream.astype(jnp.float32) * mixed.astype(jnp.float32), axis=0, keepdims=True
        )
        place = place_ref[part]

        def block(held, masked, query=query, upstream=upstream, lse=lse, delta=delta):
            scores = mm(keys[held], query)
            if masked:
                scores = jnp.where(causal(span), scores, -1e30)
            probability = jnp.exp(scores - lse)
            grad_probability = mm(values[held], upstream)
            grad_scores = (probability * (grad_probability - delta)).astype(jnp.bfloat16)
            value_sum[held] += mm_nt(probability.astype(jnp.bfloat16), upstream)
            key_sum[held] += mm_nt(grad_scores, query)
            return mm(keys_t[held], grad_scores)

        query_sum[...] = block(holder_ref[place], True)

        def earlier(j, carry, block=block):
            query_sum[...] += block(holder_ref[j], False)
            return carry

        lax.fori_loop(0, place, earlier, 0)
        for g in range(GROUP):
            dq_ref[g * HEAD : (g + 1) * HEAD, columns] = query_sum[:, g * span : (g + 1) * span]
    for c in range(spans // 2):
        for half in range(2):
            columns = slice(half * span, (half + 1) * span)
            dkv_ref[c, 0, :, columns] = key_sum[2 * c + half].T.astype(jnp.bfloat16)
            dkv_ref[c, 1, :, columns] = value_sum[2 * c + half].T.astype(jnp.bfloat16)


def attention_specs(local_rows, context_size):
    wide = pl.BlockSpec((GROUP * HEAD, local_rows), lambda b, k, *_: (k, b))
    total = pl.BlockSpec((1, GROUP, local_rows), lambda b, k, *_: (k, 0, b))
    shared = pl.BlockSpec((context_size, 2, HEAD, local_rows), lambda b, k, *_: (0, 0, k, b))
    return wide, total, shared


def attend(holder, places, queries, kv_every, local_rows):
    width, tokens = queries.shape
    context_size = kv_every.shape[0]
    span, spans = local_rows // 2, 2 * context_size
    wide, total, shared = attention_specs(local_rows, context_size)
    work = width * tokens * spans * span
    return pl.pallas_call(
        functools.partial(forward_kernel, span),
        out_shape=(
            jax.ShapeDtypeStruct((width, tokens), jnp.bfloat16),
            jax.ShapeDtypeStruct((KV_HEADS, GROUP, tokens), jnp.float32),
        ),
        grid_spec=pltpu.PrefetchScalarGridSpec(
            num_scalar_prefetch=2,
            grid=(tokens // local_rows, KV_HEADS),
            in_specs=[wide, shared],
            out_specs=(wide, total),
            scratch_shapes=[
                pltpu.VMEM((spans, span, HEAD), jnp.bfloat16),
                pltpu.VMEM((spans, HEAD, span), jnp.bfloat16),
            ],
        ),
        compiler_params=pltpu.CompilerParams(vmem_limit_bytes=32 * 1024 * 1024),
        cost_estimate=pl.CostEstimate(
            flops=16 * work, bytes_accessed=8 * width * tokens, transcendentals=work // HEAD
        ),
        name="attend",
    )(holder, places, queries, kv_every)


def attend_back(holder, places, queries, upstream, mixed, lse, kv_every, local_rows):
    width, tokens = queries.shape
    context_size = kv_every.shape[0]
    span, spans = local_rows // 2, 2 * context_size
    wide, total, shared = attention_specs(local_rows, context_size)
    work = width * tokens * spans * span
    return pl.pallas_call(
        functools.partial(backward_kernel, span),
        out_shape=(
            jax.ShapeDtypeStruct((width, tokens), jnp.float32),
            jax.ShapeDtypeStruct(kv_every.shape, jnp.bfloat16),
        ),
        grid_spec=pltpu.PrefetchScalarGridSpec(
            num_scalar_prefetch=2,
            grid=(tokens // local_rows, KV_HEADS),
            in_specs=[wide, wide, wide, total, shared],
            out_specs=(wide, shared),
            scratch_shapes=[
                pltpu.VMEM((spans, span, HEAD), jnp.bfloat16),
                pltpu.VMEM((spans, HEAD, span), jnp.bfloat16),
                pltpu.VMEM((spans, span, HEAD), jnp.bfloat16),
                pltpu.VMEM((spans, span, HEAD), jnp.float32),
                pltpu.VMEM((spans, span, HEAD), jnp.float32),
                pltpu.VMEM((HEAD, GROUP * span), jnp.float32),
            ],
        ),
        compiler_params=pltpu.CompilerParams(vmem_limit_bytes=32 * 1024 * 1024),
        cost_estimate=pl.CostEstimate(
            flops=40 * work, bytes_accessed=16 * width * tokens, transcendentals=work // HEAD
        ),
        name="attend_back",
    )(holder, places, queries, upstream, mixed, lse, kv_every)


def body(
    tokens,
    cotangent,
    span_order,
    norm_one,
    w_query,
    w_key,
    w_value,
    w_out,
    norm_two,
    w_gate,
    w_up,
    w_down,
):
    sequences, local_rows, model_width = tokens.shape
    span_size = local_rows // 2
    key_width = KV_HEADS * HEAD
    query_width = Q_HEADS * HEAD
    qkv_width = query_width + 2 * key_width
    attn_width = qkv_width + model_width
    token_count = sequences * local_rows
    inner_width = w_gate.shape[1]
    own_spans = lax.dynamic_slice_in_dim(span_order, lax.axis_index("ctx") * 2, 2)
    holder = jnp.argsort(span_order).astype(jnp.int32)
    own_places = (
        own_spans[:, None] * span_size + jnp.arange(span_size, dtype=jnp.int32)[None, :]
    ).reshape(local_rows)
    cosine, sine_part = rope_tables(jnp.tile(own_places, sequences))

    gains = jnp.stack([norm_one, norm_two], axis=1)
    attn_shard = jnp.concatenate(
        [w_query, w_key, w_value, w_out, jnp.pad(gains, ((0, 0), (0, PAD - 2)))], axis=1
    )
    attn_every = lax.all_gather(attn_shard, "fsdp", axis=0, tiled=True)
    gate_up = lax.all_gather(
        jnp.concatenate([w_gate, w_up], axis=1), "fsdp", axis=0, tiled=True
    )
    down_matrix = lax.all_gather(w_down, "fsdp", axis=0, tiled=True)
    qkv_matrix = attn_every[:, :qkv_width]
    out_matrix = attn_every[:, qkv_width:attn_width]
    gain_one = attn_every[:, attn_width].astype(jnp.float32)
    gain_two = attn_every[:, attn_width + 1].astype(jnp.float32)

    hidden_in = tokens.reshape(token_count, model_width).astype(jnp.float32)
    normed = rms_norm(hidden_in, gain_one).astype(jnp.bfloat16)
    kv_pre = product(qkv_matrix[:, query_width:], normed, "dh,nd->hn")
    keys_own = rotate(kv_pre[:key_width], cosine, sine_part).astype(jnp.bfloat16)
    kv_own = jnp.stack([keys_own, kv_pre[key_width:].astype(jnp.bfloat16)], axis=0)
    kv_every = lax.all_gather(kv_own, "ctx", axis=0, tiled=False)
    query_pre = product(qkv_matrix[:, :query_width], normed, "dh,nd->hn")
    queries = (rotate(query_pre, cosine, sine_part) * 0.125).astype(jnp.bfloat16)

    attended, lse = attend(holder, own_spans, queries, kv_every, local_rows)
    middle = hidden_in + product(attended, out_matrix, "hn,hd->nd")

    normed_two = rms_norm(middle, gain_two).astype(jnp.bfloat16)
    gate_pre = mm(normed_two, gate_up[:, :inner_width])
    up_pre = mm(normed_two, gate_up[:, inner_width:])
    inner_act = swish_gate(gate_pre, up_pre).astype(jnp.bfloat16)
    output = middle + mm(inner_act, down_matrix)

    upstream_low = cotangent.reshape(token_count, model_width)
    upstream = upstream_low.astype(jnp.float32)
    grad_inner = product(upstream_low, down_matrix, "nd,fd->nf")
    _, inner_pull = jax.vjp(swish_gate, gate_pre, up_pre)
    grad_gate_pre, grad_up_pre = inner_pull(grad_inner)
    grad_gate_up_pre = jnp.concatenate(
        [grad_gate_pre.astype(jnp.bfloat16), grad_up_pre.astype(jnp.bfloat16)], axis=1
    )
    grad_normed_two = product(grad_gate_up_pre, gate_up, "nf,df->nd")
    grad_down = product(inner_act, upstream_low, "nf,nd->fd").astype(jnp.bfloat16)
    grad_gate_up = product(normed_two, grad_gate_up_pre, "nd,nf->df").astype(jnp.bfloat16)
    down_part = lax.psum_scatter(grad_down, "fsdp", scatter_dimension=0, tiled=True)
    gate_up_part = lax.psum_scatter(grad_gate_up, "fsdp", scatter_dimension=0, tiled=True)

    _, second_pull = jax.vjp(rms_norm, middle, gain_two)
    grad_middle_norm, grad_gain_two = second_pull(grad_normed_two)
    grad_middle = upstream + grad_middle_norm
    middle_low = grad_middle.astype(jnp.bfloat16)
    grad_attended = product(out_matrix, middle_low, "hd,nd->hn").astype(jnp.bfloat16)

    query_grads, kv_grads = attend_back(
        holder, own_spans, queries, grad_attended, attended, lse, kv_every, local_rows
    )
    kv_mine = lax.psum_scatter(kv_grads, "ctx", scatter_dimension=0, tiled=False)
    grad_out = product(attended, middle_low, "hn,nd->hd")
    query_low = (rotate(query_grads, cosine, -sine_part) * 0.125).astype(jnp.bfloat16)
    key_low = rotate(kv_mine[0].astype(jnp.float32), cosine, -sine_part).astype(jnp.bfloat16)
    qkv_low = jnp.concatenate([query_low, key_low, kv_mine[1]], axis=0)
    grad_qkv = product(normed, qkv_low, "nd,hn->dh")
    grad_normed = product(qkv_low, qkv_matrix, "hn,dh->nd")
    _, first_pull = jax.vjp(rms_norm, hidden_in, gain_one)
    grad_hidden_norm, grad_gain_one = first_pull(grad_normed)
    grad_input = grad_middle + grad_hidden_norm

    grad_gains = jnp.pad(
        jnp.stack([grad_gain_one, grad_gain_two], axis=1), ((0, 0), (0, PAD - 2))
    )
    attn_grads = jnp.concatenate([grad_qkv, grad_out, grad_gains], axis=1).astype(jnp.bfloat16)
    attn_part = lax.psum_scatter(attn_grads, "fsdp", scatter_dimension=0, tiled=True)
    down_sum = lax.psum(down_part, "ctx").astype(jnp.float32)
    gate_up_sum = lax.psum(gate_up_part, "ctx").astype(jnp.float32)
    attn_sum = lax.psum(attn_part, "ctx").astype(jnp.float32)
    key_start = query_width
    value_start = query_width + key_width
    return (
        output.astype(jnp.bfloat16).reshape(tokens.shape),
        grad_input.reshape(tokens.shape),
        attn_sum[:, attn_width],
        attn_sum[:, :key_start],
        attn_sum[:, key_start:value_start],
        attn_sum[:, value_start:qkv_width],
        attn_sum[:, qkv_width:attn_width],
        attn_sum[:, attn_width + 1],
        gate_up_sum[:, :inner_width],
        gate_up_sum[:, inner_width:],
        down_sum,
    )


def solution(mesh):
    in_specs = (
        P("fsdp", "ctx", None),
        P("fsdp", "ctx", None),
        P(),
        P("fsdp"),
        P("fsdp", None),
        P("fsdp", None),
        P("fsdp", None),
        P("fsdp", None),
        P("fsdp"),
        P("fsdp", None),
        P("fsdp", None),
        P("fsdp", None),
    )
    out_specs = (
        P("fsdp", "ctx", None),
        P("fsdp", "ctx", None),
        P("fsdp"),
        P("fsdp", None),
        P("fsdp", None),
        P("fsdp", None),
        P("fsdp", None),
        P("fsdp"),
        P("fsdp", None),
        P("fsdp", None),
        P("fsdp", None),
    )
    return jax.shard_map(body, mesh=mesh, in_specs=in_specs, out_specs=out_specs, check_vma=False)
```

```python
import functools

import jax
import jax.numpy as jnp
from jax import lax
from jax.experimental import pallas as pl
from jax.experimental.pallas import tpu as pltpu
from jax.sharding import PartitionSpec as P

Q_HEADS = 9
KV_HEADS = 3
HEAD = 64
GROUP = Q_HEADS // KV_HEADS
PAD = 128
GRAD_PAD = 512

epsilon = 1e-05
rope_base = 100000.0


def rms_norm(values, gain_vector):
    scaling = lax.rsqrt(jnp.mean(values * values, axis=-1, keepdims=True) + epsilon)
    return values * scaling * gain_vector


def rope_tables(positions):
    half_size = HEAD // 2
    frequency = rope_base ** (-2.0 * jnp.arange(half_size, dtype=jnp.float32) / HEAD)
    angles = frequency[:, None] * positions.astype(jnp.float32)[None, :]
    return jnp.cos(angles), jnp.sin(angles)


def rotate(features, cosine, sine_part):
    count = features.shape[1]
    pairs = features.reshape(-1, 2, HEAD // 2, count)
    first, second = pairs[:, 0], pairs[:, 1]
    turned = jnp.stack(
        [first * cosine - second * sine_part, second * cosine + first * sine_part], axis=1
    )
    return turned.reshape(features.shape)


def product(left_side, right_side, pattern):
    return jnp.einsum(pattern, left_side, right_side, preferred_element_type=jnp.float32)


def swish_gate(gate_in, upper_in):
    return jax.nn.silu(gate_in) * upper_in


def mm(left_side, right_side):
    return jnp.dot(left_side, right_side, preferred_element_type=jnp.float32)


def mm_nt(left_side, right_side):
    return lax.dot_general(
        left_side, right_side, (((1,), (1,)), ((), ())), preferred_element_type=jnp.float32
    )


def causal(span):
    shape = (span, GROUP * span)
    key_at = lax.broadcasted_iota(jnp.int32, shape, 0)
    query_at = lax.rem(lax.broadcasted_iota(jnp.int32, shape, 1), span)
    return key_at <= query_at


def heads_side_by_side(ref, part, span):
    columns = slice(part * span, (part + 1) * span)
    return jnp.concatenate(
        [ref[g * HEAD : (g + 1) * HEAD, columns] for g in range(GROUP)], axis=1
    )


def forward_kernel(span, holder_ref, place_ref, q_ref, kv_ref, o_ref, lse_ref, keys, values):
    spans = keys.shape[0]
    for c in range(spans // 2):
        for half in range(2):
            columns = slice(half * span, (half + 1) * span)
            keys[2 * c + half] = kv_ref[c, 0, :, columns].T
            values[2 * c + half] = kv_ref[c, 1, :, columns]
    for part in range(2):
        query = heads_side_by_side(q_ref, part, span)
        place = place_ref[part]
        own = holder_ref[place]
        scores = jnp.where(causal(span), mm(keys[own], query), -1e30)
        top = jnp.max(scores, axis=0, keepdims=True)
        raised = jnp.exp(scores - top)
        total = jnp.sum(raised, axis=0, keepdims=True)
        mixed = mm(values[own], raised.astype(jnp.bfloat16))

        def earlier(j, carry, query=query):
            top, total, mixed = carry
            held = holder_ref[j]
            scores = mm(keys[held], query)
            new_top = jnp.maximum(top, jnp.max(scores, axis=0, keepdims=True))
            shrink = jnp.exp(top - new_top)
            raised = jnp.exp(scores - new_top)
            total = total * shrink + jnp.sum(raised, axis=0, keepdims=True)
            mixed = mixed * shrink + mm(values[held], raised.astype(jnp.bfloat16))
            return new_top, total, mixed

        top, total, mixed = lax.fori_loop(0, place, earlier, (top, total, mixed))
        mixed = mixed / total
        lse = top + jnp.log(total)
        for g in range(GROUP):
            source = slice(g * span, (g + 1) * span)
            columns = slice(part * span, (part + 1) * span)
            o_ref[g * HEAD : (g + 1) * HEAD, columns] = mixed[:, source].astype(jnp.bfloat16)
            lse_ref[0, g : g + 1, columns] = lse[:, source]


def backward_kernel(
    span, holder_ref, place_ref, q_ref, do_ref, o_ref, lse_ref, kv_ref,
    dq_ref, dkv_ref, keys, keys_t, values, key_sum, value_sum, query_sum,
):
    spans = keys.shape[0]
    for c in range(spans // 2):
        for half in range(2):
            columns = slice(half * span, (half + 1) * span)
            keys[2 * c + half] = kv_ref[c, 0, :, columns].T
            keys_t[2 * c + half] = kv_ref[c, 0, :, columns]
            values[2 * c + half] = kv_ref[c, 1, :, columns].T
    key_sum[...] = jnp.zeros_like(key_sum)
    value_sum[...] = jnp.zeros_like(value_sum)
    for part in range(2):
        query = heads_side_by_side(q_ref, part, span)
        upstream = heads_side_by_side(do_ref, part, span)
        mixed = heads_side_by_side(o_ref, part, span)
        columns = slice(part * span, (part + 1) * span)
        lse = jnp.concatenate([lse_ref[0, g : g + 1, columns] for g in range(GROUP)], axis=1)
        delta = jnp.sum(
            upstream.astype(jnp.float32) * mixed.astype(jnp.float32), axis=0, keepdims=True
        )
        place = place_ref[part]

        def block(held, masked, query=query, upstream=upstream, lse=lse, delta=delta):
            scores = mm(keys[held], query)
            if masked:
                scores = jnp.where(causal(span), scores, -1e30)
            probability = jnp.exp(scores - lse)
            grad_probability = mm(values[held], upstream)
            grad_scores = (probability * (grad_probability - delta)).astype(jnp.bfloat16)
            value_sum[held] += mm_nt(probability.astype(jnp.bfloat16), upstream)
            key_sum[held] += mm_nt(grad_scores, query)
            return mm(keys_t[held], grad_scores)

        query_sum[...] = block(holder_ref[place], True)

        def earlier(j, carry, block=block):
            query_sum[...] += block(holder_ref[j], False)
            return carry

        lax.fori_loop(0, place, earlier, 0)
        for g in range(GROUP):
            dq_ref[g * HEAD : (g + 1) * HEAD, columns] = query_sum[:, g * span : (g + 1) * span]
    for c in range(spans // 2):
        for half in range(2):
            columns = slice(half * span, (half + 1) * span)
            dkv_ref[c, 0, :, columns] = key_sum[2 * c + half].T.astype(jnp.bfloat16)
            dkv_ref[c, 1, :, columns] = value_sum[2 * c + half].T.astype(jnp.bfloat16)


def attention_specs(local_rows, context_size):
    wide = pl.BlockSpec((GROUP * HEAD, local_rows), lambda b, k, *_: (k, b))
    total = pl.BlockSpec((1, GROUP, local_rows), lambda b, k, *_: (k, 0, b))
    shared = pl.BlockSpec((context_size, 2, HEAD, local_rows), lambda b, k, *_: (0, 0, k, b))
    return wide, total, shared


def attend(holder, places, queries, kv_every, local_rows):
    width, tokens = queries.shape
    context_size = kv_every.shape[0]
    span, spans = local_rows // 2, 2 * context_size
    wide, total, shared = attention_specs(local_rows, context_size)
    work = width * tokens * spans * span
    return pl.pallas_call(
        functools.partial(forward_kernel, span),
        out_shape=(
            jax.ShapeDtypeStruct((width, tokens), jnp.bfloat16),
            jax.ShapeDtypeStruct((KV_HEADS, GROUP, tokens), jnp.float32),
        ),
        grid_spec=pltpu.PrefetchScalarGridSpec(
            num_scalar_prefetch=2,
            grid=(tokens // local_rows, KV_HEADS),
            in_specs=[wide, shared],
            out_specs=(wide, total),
            scratch_shapes=[
                pltpu.VMEM((spans, span, HEAD), jnp.bfloat16),
                pltpu.VMEM((spans, HEAD, span), jnp.bfloat16),
            ],
        ),
        compiler_params=pltpu.CompilerParams(vmem_limit_bytes=32 * 1024 * 1024),
        cost_estimate=pl.CostEstimate(
            flops=16 * work, bytes_accessed=8 * width * tokens, transcendentals=work // HEAD
        ),
        name="attend",
    )(holder, places, queries, kv_every)


def attend_back(holder, places, queries, upstream, mixed, lse, kv_every, local_rows):
    width, tokens = queries.shape
    context_size = kv_every.shape[0]
    span, spans = local_rows // 2, 2 * context_size
    wide, total, shared = attention_specs(local_rows, context_size)
    work = width * tokens * spans * span
    return pl.pallas_call(
        functools.partial(backward_kernel, span),
        out_shape=(
            jax.ShapeDtypeStruct((width, tokens), jnp.float32),
            jax.ShapeDtypeStruct(kv_every.shape, jnp.bfloat16),
        ),
        grid_spec=pltpu.PrefetchScalarGridSpec(
            num_scalar_prefetch=2,
            grid=(tokens // local_rows, KV_HEADS),
            in_specs=[wide, wide, wide, total, shared],
            out_specs=(wide, shared),
            scratch_shapes=[
                pltpu.VMEM((spans, span, HEAD), jnp.bfloat16),
                pltpu.VMEM((spans, HEAD, span), jnp.bfloat16),
                pltpu.VMEM((spans, span, HEAD), jnp.bfloat16),
                pltpu.VMEM((spans, span, HEAD), jnp.float32),
                pltpu.VMEM((spans, span, HEAD), jnp.float32),
                pltpu.VMEM((HEAD, GROUP * span), jnp.float32),
            ],
        ),
        compiler_params=pltpu.CompilerParams(vmem_limit_bytes=32 * 1024 * 1024),
        cost_estimate=pl.CostEstimate(
            flops=40 * work, bytes_accessed=16 * width * tokens, transcendentals=work // HEAD
        ),
        name="attend_back",
    )(holder, places, queries, upstream, mixed, lse, kv_every)


def swap(values, bit):
    size = lax.axis_size("ctx")
    return lax.ppermute(values, "ctx", [(i, i ^ bit) for i in range(size)])


def halve(values, bit):
    side = (lax.axis_index("ctx") // bit) % 2
    away = lax.dynamic_index_in_dim(values, 1 - side, 0, keepdims=False)
    mine = lax.dynamic_index_in_dim(values, side, 0, keepdims=False)
    came = swap(away, bit)
    return (mine.astype(jnp.float32) + came.astype(jnp.float32)).astype(values.dtype)


def join(values, bit):
    side = (lax.axis_index("ctx") // bit) % 2
    came = swap(values, bit)
    first = jnp.where(side == 0, values, came)
    second = jnp.where(side == 0, came, values)
    return jnp.stack([first, second], axis=0)


def scatter_ctx(values):
    pairs = values.reshape((2, 2) + values.shape[1:])
    return halve(halve(jnp.swapaxes(pairs, 0, 1), 1), 2)


def gather_ctx(values):
    joined = join(join(values, 2), 1)
    return jnp.swapaxes(joined, 0, 1).reshape((4,) + values.shape)


def scatter_fsdp(values):
    size = lax.axis_size("fsdp")
    if size > 8:
        return lax.psum_scatter(values, "fsdp", scatter_dimension=0, tiled=False)
    me = lax.axis_index("fsdp")
    total = lax.dynamic_index_in_dim(values, me, 0, keepdims=False).astype(jnp.float32)
    for step in range(1, size):
        piece = lax.dynamic_index_in_dim(values, (me + step) % size, 0, keepdims=False)
        came = lax.ppermute(piece, "fsdp", [(i, (i + step) % size) for i in range(size)])
        total = total + came.astype(jnp.float32)
    return total.astype(values.dtype)


def gather_fsdp(values):
    size = lax.axis_size("fsdp")
    if size > 8:
        return lax.all_gather(values, "fsdp", axis=0, tiled=False)
    me = lax.axis_index("fsdp")
    every = jnp.zeros((size,) + values.shape, values.dtype)
    every = lax.dynamic_update_index_in_dim(every, values, me, 0)
    for step in range(1, size):
        came = lax.ppermute(values, "fsdp", [(i, (i + step) % size) for i in range(size)])
        every = lax.dynamic_update_index_in_dim(every, came, (me - step) % size, 0)
    return every


def own_quarter(values):
    return lax.dynamic_index_in_dim(values, lax.axis_index("ctx"), 0, keepdims=False)


def column_quarters(values):
    rows, width = values.shape
    return jnp.stack([values[:, q * width // 4 : (q + 1) * width // 4] for q in range(4)], axis=0)


def gather_columns(shard):
    quarter = gather_fsdp(own_quarter(column_quarters(shard)))
    every = gather_ctx(quarter.reshape(-1, quarter.shape[-1]))
    return jnp.concatenate([every[q] for q in range(4)], axis=1)


def gather_rows(shard):
    rows, width = shard.shape
    quarter = gather_fsdp(own_quarter(shard.reshape(4, rows // 4, width)))
    every = gather_ctx(quarter)
    return jnp.swapaxes(every, 0, 1).reshape(-1, width)


def reduce_columns(values):
    size = lax.axis_size("fsdp")
    quarter = scatter_ctx(column_quarters(values))
    quarter = quarter.reshape(size, -1, quarter.shape[-1])
    every = gather_ctx(scatter_fsdp(quarter))
    return jnp.concatenate([every[q] for q in range(4)], axis=1).astype(jnp.float32)


def reduce_rows(values):
    size = lax.axis_size("fsdp")
    width = values.shape[-1]
    quarters = jnp.swapaxes(values.reshape(size, 4, -1, width), 0, 1)
    every = gather_ctx(scatter_fsdp(scatter_ctx(quarters)))
    return every.reshape(-1, width).astype(jnp.float32)


def body(
    tokens,
    cotangent,
    span_order,
    norm_one,
    w_query,
    w_key,
    w_value,
    w_out,
    norm_two,
    w_gate,
    w_up,
    w_down,
):
    sequences, local_rows, model_width = tokens.shape
    span_size = local_rows // 2
    key_width = KV_HEADS * HEAD
    query_width = Q_HEADS * HEAD
    qkv_width = query_width + 2 * key_width
    attn_width = qkv_width + model_width
    token_count = sequences * local_rows
    inner_width = w_gate.shape[1]
    own_spans = lax.dynamic_slice_in_dim(span_order, lax.axis_index("ctx") * 2, 2)
    holder = jnp.argsort(span_order).astype(jnp.int32)
    own_places = (
        own_spans[:, None] * span_size + jnp.arange(span_size, dtype=jnp.int32)[None, :]
    ).reshape(local_rows)
    cosine, sine_part = rope_tables(jnp.tile(own_places, sequences))

    gains = jnp.stack([norm_one, norm_two], axis=1)
    attn_shard = jnp.concatenate(
        [w_query, w_key, w_value, w_out, jnp.pad(gains, ((0, 0), (0, PAD - 2)))], axis=1
    )
    attn_every = lax.all_gather(attn_shard, "fsdp", axis=0, tiled=True)
    gate_up = gather_columns(jnp.concatenate([w_gate, w_up], axis=1))
    down_matrix = gather_rows(w_down)
    qkv_matrix = attn_every[:, :qkv_width]
    out_matrix = attn_every[:, qkv_width:attn_width]
    gain_one = attn_every[:, attn_width].astype(jnp.float32)
    gain_two = attn_every[:, attn_width + 1].astype(jnp.float32)

    hidden_in = tokens.reshape(token_count, model_width).astype(jnp.float32)
    normed = rms_norm(hidden_in, gain_one).astype(jnp.bfloat16)
    kv_pre = product(qkv_matrix[:, query_width:], normed, "dh,nd->hn")
    keys_own = rotate(kv_pre[:key_width], cosine, sine_part).astype(jnp.bfloat16)
    kv_own = jnp.stack([keys_own, kv_pre[key_width:].astype(jnp.bfloat16)], axis=0)
    kv_every = lax.all_gather(kv_own, "ctx", axis=0, tiled=False)
    query_pre = product(qkv_matrix[:, :query_width], normed, "dh,nd->hn")
    queries = (rotate(query_pre, cosine, sine_part) * 0.125).astype(jnp.bfloat16)

    attended, lse = attend(holder, own_spans, queries, kv_every, local_rows)
    middle = hidden_in + product(attended, out_matrix, "hn,hd->nd")

    normed_two = rms_norm(middle, gain_two).astype(jnp.bfloat16)
    gate_pre = mm(normed_two, gate_up[:, :inner_width])
    up_pre = mm(normed_two, gate_up[:, inner_width:])
    inner_act = swish_gate(gate_pre, up_pre).astype(jnp.bfloat16)
    output = middle + mm(inner_act, down_matrix)

    upstream_low = cotangent.reshape(token_count, model_width)
    upstream = upstream_low.astype(jnp.float32)
    grad_inner = product(upstream_low, down_matrix, "nd,fd->nf")
    _, inner_pull = jax.vjp(swish_gate, gate_pre, up_pre)
    grad_gate_pre, grad_up_pre = inner_pull(grad_inner)
    grad_gate_up_pre = jnp.concatenate(
        [grad_gate_pre.astype(jnp.bfloat16), grad_up_pre.astype(jnp.bfloat16)], axis=1
    )
    grad_normed_two = product(grad_gate_up_pre, gate_up, "nf,df->nd")
    grad_down = product(inner_act, upstream_low, "nf,nd->fd").astype(jnp.bfloat16)
    grad_gate_up = product(normed_two, grad_gate_up_pre, "nd,nf->df").astype(jnp.bfloat16)
    down_sum = reduce_rows(grad_down)
    gate_up_sum = reduce_columns(grad_gate_up)

    _, second_pull = jax.vjp(rms_norm, middle, gain_two)
    grad_middle_norm, grad_gain_two = second_pull(grad_normed_two)
    grad_middle = upstream + grad_middle_norm
    middle_low = grad_middle.astype(jnp.bfloat16)
    grad_attended = product(out_matrix, middle_low, "hd,nd->hn").astype(jnp.bfloat16)

    query_grads, kv_grads = attend_back(
        holder, own_spans, queries, grad_attended, attended, lse, kv_every, local_rows
    )
    kv_mine = scatter_ctx(kv_grads)
    grad_out = product(attended, middle_low, "hn,nd->hd")
    query_low = (rotate(query_grads, cosine, -sine_part) * 0.125).astype(jnp.bfloat16)
    key_low = rotate(kv_mine[0].astype(jnp.float32), cosine, -sine_part).astype(jnp.bfloat16)
    qkv_low = jnp.concatenate([query_low, key_low, kv_mine[1]], axis=0)
    grad_qkv = product(normed, qkv_low, "nd,hn->dh")
    grad_normed = product(qkv_low, qkv_matrix, "hn,dh->nd")
    _, first_pull = jax.vjp(rms_norm, hidden_in, gain_one)
    grad_hidden_norm, grad_gain_one = first_pull(grad_normed)
    grad_input = grad_middle + grad_hidden_norm

    grad_gains = jnp.pad(
        jnp.stack([grad_gain_one, grad_gain_two], axis=1), ((0, 0), (0, GRAD_PAD - 2))
    )
    attn_grads = jnp.concatenate([grad_qkv, grad_out, grad_gains], axis=1).astype(jnp.bfloat16)
    attn_sum = reduce_columns(attn_grads)
    key_start = query_width
    value_start = query_width + key_width
    return (
        output.astype(jnp.bfloat16).reshape(tokens.shape),
        grad_input.reshape(tokens.shape),
        attn_sum[:, attn_width],
        attn_sum[:, :key_start],
        attn_sum[:, key_start:value_start],
        attn_sum[:, value_start:qkv_width],
        attn_sum[:, qkv_width:attn_width],
        attn_sum[:, attn_width + 1],
        gate_up_sum[:, :inner_width],
        gate_up_sum[:, inner_width:],
        down_sum,
    )


def solution(mesh):
    in_specs = (
        P("fsdp", "ctx", None),
        P("fsdp", "ctx", None),
        P(),
        P("fsdp"),
        P("fsdp", None),
        P("fsdp", None),
        P("fsdp", None),
        P("fsdp", None),
        P("fsdp"),
        P("fsdp", None),
        P("fsdp", None),
        P("fsdp", None),
    )
    out_specs = (
        P("fsdp", "ctx", None),
        P("fsdp", "ctx", None),
        P("fsdp"),
        P("fsdp", None),
        P("fsdp", None),
        P("fsdp", None),
        P("fsdp", None),
        P("fsdp"),
        P("fsdp", None),
        P("fsdp", None),
        P("fsdp", None),
    )
    return jax.shard_map(body, mesh=mesh, in_specs=in_specs, out_specs=out_specs, check_vma=False)
```

```python
import functools

import jax
import jax.numpy as jnp
from jax import lax
from jax.experimental import pallas as pl
from jax.experimental.pallas import tpu as pltpu
from jax.sharding import PartitionSpec as P

Q_HEADS = 9
KV_HEADS = 3
HEAD = 64
GROUP = Q_HEADS // KV_HEADS
PAD = 128
GRAD_PAD = 512

epsilon = 1e-05
rope_base = 100000.0


def rms_norm(values, gain_vector):
    scaling = lax.rsqrt(jnp.mean(values * values, axis=-1, keepdims=True) + epsilon)
    return values * scaling * gain_vector


def rope_tables(positions):
    half_size = HEAD // 2
    frequency = rope_base ** (-2.0 * jnp.arange(half_size, dtype=jnp.float32) / HEAD)
    angles = frequency[:, None] * positions.astype(jnp.float32)[None, :]
    return jnp.cos(angles), jnp.sin(angles)


def rotate(features, cosine, sine_part):
    count = features.shape[1]
    pairs = features.reshape(-1, 2, HEAD // 2, count)
    first, second = pairs[:, 0], pairs[:, 1]
    turned = jnp.stack(
        [first * cosine - second * sine_part, second * cosine + first * sine_part], axis=1
    )
    return turned.reshape(features.shape)


def product(left_side, right_side, pattern):
    return jnp.einsum(pattern, left_side, right_side, preferred_element_type=jnp.float32)


def swish_gate(gate_in, upper_in):
    return jax.nn.silu(gate_in) * upper_in


def mm(left_side, right_side):
    return jnp.dot(left_side, right_side, preferred_element_type=jnp.float32)


def mm_nt(left_side, right_side):
    return lax.dot_general(
        left_side, right_side, (((1,), (1,)), ((), ())), preferred_element_type=jnp.float32
    )


def causal(span):
    shape = (span, GROUP * span)
    key_at = lax.broadcasted_iota(jnp.int32, shape, 0)
    query_at = lax.rem(lax.broadcasted_iota(jnp.int32, shape, 1), span)
    return key_at <= query_at


def heads_side_by_side(ref, part, span):
    columns = slice(part * span, (part + 1) * span)
    return jnp.concatenate(
        [ref[g * HEAD : (g + 1) * HEAD, columns] for g in range(GROUP)], axis=1
    )


def forward_kernel(span, holder_ref, place_ref, q_ref, kv_ref, o_ref, lse_ref, keys, values):
    spans = keys.shape[0]
    for c in range(spans // 2):
        for half in range(2):
            columns = slice(half * span, (half + 1) * span)
            keys[2 * c + half] = kv_ref[c, 0, :, columns].T
            values[2 * c + half] = kv_ref[c, 1, :, columns]
    for part in range(2):
        query = heads_side_by_side(q_ref, part, span)
        place = place_ref[part]
        own = holder_ref[place]
        scores = jnp.where(causal(span), mm(keys[own], query), -1e30)
        top = jnp.max(scores, axis=0, keepdims=True)
        raised = jnp.exp(scores - top)
        total = jnp.sum(raised, axis=0, keepdims=True)
        mixed = mm(values[own], raised.astype(jnp.bfloat16))

        def earlier(j, carry, query=query):
            top, total, mixed = carry
            held = holder_ref[j]
            scores = mm(keys[held], query)
            new_top = jnp.maximum(top, jnp.max(scores, axis=0, keepdims=True))
            shrink = jnp.exp(top - new_top)
            raised = jnp.exp(scores - new_top)
            total = total * shrink + jnp.sum(raised, axis=0, keepdims=True)
            mixed = mixed * shrink + mm(values[held], raised.astype(jnp.bfloat16))
            return new_top, total, mixed

        def two_earlier(j, carry, query=query):
            top, total, mixed = carry
            one, other = holder_ref[2 * j], holder_ref[2 * j + 1]
            scores_one = mm(keys[one], query)
            scores_other = mm(keys[other], query)
            new_top = jnp.maximum(
                top, jnp.max(jnp.maximum(scores_one, scores_other), axis=0, keepdims=True)
            )
            shrink = jnp.exp(top - new_top)
            raised_one = jnp.exp(scores_one - new_top)
            raised_other = jnp.exp(scores_other - new_top)
            total = total * shrink + jnp.sum(raised_one + raised_other, axis=0, keepdims=True)
            mixed = (
                mixed * shrink
                + mm(values[one], raised_one.astype(jnp.bfloat16))
                + mm(values[other], raised_other.astype(jnp.bfloat16))
            )
            return new_top, total, mixed

        paired = place // 2
        state = lax.fori_loop(0, paired, two_earlier, (top, total, mixed))
        top, total, mixed = lax.fori_loop(2 * paired, place, earlier, state)
        mixed = mixed / total
        lse = top + jnp.log(total)
        for g in range(GROUP):
            source = slice(g * span, (g + 1) * span)
            columns = slice(part * span, (part + 1) * span)
            o_ref[g * HEAD : (g + 1) * HEAD, columns] = mixed[:, source].astype(jnp.bfloat16)
            lse_ref[0, g : g + 1, columns] = lse[:, source]


def backward_kernel(
    span, holder_ref, place_ref, q_ref, do_ref, o_ref, lse_ref, kv_ref,
    dq_ref, dkv_ref, keys, keys_t, values, key_sum, value_sum, query_sum,
):
    spans = keys.shape[0]
    for c in range(spans // 2):
        for half in range(2):
            columns = slice(half * span, (half + 1) * span)
            keys[2 * c + half] = kv_ref[c, 0, :, columns].T
            keys_t[2 * c + half] = kv_ref[c, 0, :, columns]
            values[2 * c + half] = kv_ref[c, 1, :, columns].T
    key_sum[...] = jnp.zeros_like(key_sum)
    value_sum[...] = jnp.zeros_like(value_sum)
    for part in range(2):
        query = heads_side_by_side(q_ref, part, span)
        upstream = heads_side_by_side(do_ref, part, span)
        mixed = heads_side_by_side(o_ref, part, span)
        columns = slice(part * span, (part + 1) * span)
        lse = jnp.concatenate([lse_ref[0, g : g + 1, columns] for g in range(GROUP)], axis=1)
        delta = jnp.sum(
            upstream.astype(jnp.float32) * mixed.astype(jnp.float32), axis=0, keepdims=True
        )
        place = place_ref[part]

        def block(held, masked, query=query, upstream=upstream, lse=lse, delta=delta):
            scores = mm(keys[held], query)
            if masked:
                scores = jnp.where(causal(span), scores, -1e30)
            probability = jnp.exp(scores - lse)
            grad_probability = mm(values[held], upstream)
            grad_scores = (probability * (grad_probability - delta)).astype(jnp.bfloat16)
            value_sum[held] += mm_nt(probability.astype(jnp.bfloat16), upstream)
            key_sum[held] += mm_nt(grad_scores, query)
            return mm(keys_t[held], grad_scores)

        query_sum[...] = block(holder_ref[place], True)

        def earlier(j, carry, block=block):
            query_sum[...] += block(holder_ref[j], False)
            return carry

        lax.fori_loop(0, place, earlier, 0)
        for g in range(GROUP):
            dq_ref[g * HEAD : (g + 1) * HEAD, columns] = query_sum[:, g * span : (g + 1) * span]
    for c in range(spans // 2):
        for half in range(2):
            columns = slice(half * span, (half + 1) * span)
            dkv_ref[c, 0, :, columns] = key_sum[2 * c + half].T.astype(jnp.bfloat16)
            dkv_ref[c, 1, :, columns] = value_sum[2 * c + half].T.astype(jnp.bfloat16)


def attention_specs(local_rows, context_size):
    wide = pl.BlockSpec((GROUP * HEAD, local_rows), lambda b, k, *_: (k, b))
    total = pl.BlockSpec((1, GROUP, local_rows), lambda b, k, *_: (k, 0, b))
    shared = pl.BlockSpec((context_size, 2, HEAD, local_rows), lambda b, k, *_: (0, 0, k, b))
    return wide, total, shared


def attend(holder, places, queries, kv_every, local_rows):
    width, tokens = queries.shape
    context_size = kv_every.shape[0]
    span, spans = local_rows // 2, 2 * context_size
    wide, total, shared = attention_specs(local_rows, context_size)
    work = width * tokens * spans * span
    return pl.pallas_call(
        functools.partial(forward_kernel, span),
        out_shape=(
            jax.ShapeDtypeStruct((width, tokens), jnp.bfloat16),
            jax.ShapeDtypeStruct((KV_HEADS, GROUP, tokens), jnp.float32),
        ),
        grid_spec=pltpu.PrefetchScalarGridSpec(
            num_scalar_prefetch=2,
            grid=(tokens // local_rows, KV_HEADS),
            in_specs=[wide, shared],
            out_specs=(wide, total),
            scratch_shapes=[
                pltpu.VMEM((spans, span, HEAD), jnp.bfloat16),
                pltpu.VMEM((spans, HEAD, span), jnp.bfloat16),
            ],
        ),
        compiler_params=pltpu.CompilerParams(vmem_limit_bytes=32 * 1024 * 1024),
        cost_estimate=pl.CostEstimate(
            flops=16 * work, bytes_accessed=8 * width * tokens, transcendentals=work // HEAD
        ),
        name="attend",
    )(holder, places, queries, kv_every)


def attend_back(holder, places, queries, upstream, mixed, lse, kv_every, local_rows):
    width, tokens = queries.shape
    context_size = kv_every.shape[0]
    span, spans = local_rows // 2, 2 * context_size
    wide, total, shared = attention_specs(local_rows, context_size)
    work = width * tokens * spans * span
    return pl.pallas_call(
        functools.partial(backward_kernel, span),
        out_shape=(
            jax.ShapeDtypeStruct((width, tokens), jnp.float32),
            jax.ShapeDtypeStruct(kv_every.shape, jnp.bfloat16),
        ),
        grid_spec=pltpu.PrefetchScalarGridSpec(
            num_scalar_prefetch=2,
            grid=(tokens // local_rows, KV_HEADS),
            in_specs=[wide, wide, wide, total, shared],
            out_specs=(wide, shared),
            scratch_shapes=[
                pltpu.VMEM((spans, span, HEAD), jnp.bfloat16),
                pltpu.VMEM((spans, HEAD, span), jnp.bfloat16),
                pltpu.VMEM((spans, span, HEAD), jnp.bfloat16),
                pltpu.VMEM((spans, span, HEAD), jnp.float32),
                pltpu.VMEM((spans, span, HEAD), jnp.float32),
                pltpu.VMEM((HEAD, GROUP * span), jnp.float32),
            ],
        ),
        compiler_params=pltpu.CompilerParams(vmem_limit_bytes=32 * 1024 * 1024),
        cost_estimate=pl.CostEstimate(
            flops=40 * work, bytes_accessed=16 * width * tokens, transcendentals=work // HEAD
        ),
        name="attend_back",
    )(holder, places, queries, upstream, mixed, lse, kv_every)


def swap(values, bit):
    size = lax.axis_size("ctx")
    return lax.ppermute(values, "ctx", [(i, i ^ bit) for i in range(size)])


def halve(values, bit):
    side = (lax.axis_index("ctx") // bit) % 2
    away = lax.dynamic_index_in_dim(values, 1 - side, 0, keepdims=False)
    mine = lax.dynamic_index_in_dim(values, side, 0, keepdims=False)
    came = swap(away, bit)
    return (mine.astype(jnp.float32) + came.astype(jnp.float32)).astype(values.dtype)


def join(values, bit):
    side = (lax.axis_index("ctx") // bit) % 2
    came = swap(values, bit)
    first = jnp.where(side == 0, values, came)
    second = jnp.where(side == 0, came, values)
    return jnp.stack([first, second], axis=0)


def scatter_ctx(values):
    pairs = values.reshape((2, 2) + values.shape[1:])
    return halve(halve(jnp.swapaxes(pairs, 0, 1), 1), 2)


def gather_ctx(values):
    joined = join(join(values, 2), 1)
    return jnp.swapaxes(joined, 0, 1).reshape((4,) + values.shape)


def scatter_fsdp(values):
    size = lax.axis_size("fsdp")
    if size > 8:
        return lax.psum_scatter(values, "fsdp", scatter_dimension=0, tiled=False)
    me = lax.axis_index("fsdp")
    total = lax.dynamic_index_in_dim(values, me, 0, keepdims=False).astype(jnp.float32)
    for step in range(1, size):
        piece = lax.dynamic_index_in_dim(values, (me + step) % size, 0, keepdims=False)
        came = lax.ppermute(piece, "fsdp", [(i, (i + step) % size) for i in range(size)])
        total = total + came.astype(jnp.float32)
    return total.astype(values.dtype)


def gather_fsdp(values):
    size = lax.axis_size("fsdp")
    if size > 8:
        return lax.all_gather(values, "fsdp", axis=0, tiled=False)
    me = lax.axis_index("fsdp")
    every = jnp.zeros((size,) + values.shape, values.dtype)
    every = lax.dynamic_update_index_in_dim(every, values, me, 0)
    for step in range(1, size):
        came = lax.ppermute(values, "fsdp", [(i, (i + step) % size) for i in range(size)])
        every = lax.dynamic_update_index_in_dim(every, came, (me - step) % size, 0)
    return every


def own_quarter(values):
    return lax.dynamic_index_in_dim(values, lax.axis_index("ctx"), 0, keepdims=False)


def column_quarters(values):
    rows, width = values.shape
    return jnp.stack([values[:, q * width // 4 : (q + 1) * width // 4] for q in range(4)], axis=0)


def gather_columns(shard):
    quarter = gather_fsdp(own_quarter(column_quarters(shard)))
    every = gather_ctx(quarter.reshape(-1, quarter.shape[-1]))
    return jnp.concatenate([every[q] for q in range(4)], axis=1)


def gather_rows(shard):
    rows, width = shard.shape
    quarter = gather_fsdp(own_quarter(shard.reshape(4, rows // 4, width)))
    every = gather_ctx(quarter)
    return jnp.swapaxes(every, 0, 1).reshape(-1, width)


def reduce_columns(values):
    size = lax.axis_size("fsdp")
    quarter = scatter_ctx(column_quarters(values))
    quarter = quarter.reshape(size, -1, quarter.shape[-1])
    every = gather_ctx(scatter_fsdp(quarter))
    return jnp.concatenate([every[q] for q in range(4)], axis=1).astype(jnp.float32)


def body(
    tokens,
    cotangent,
    span_order,
    norm_one,
    w_query,
    w_key,
    w_value,
    w_out,
    norm_two,
    w_gate,
    w_up,
    w_down,
):
    sequences, local_rows, model_width = tokens.shape
    span_size = local_rows // 2
    key_width = KV_HEADS * HEAD
    query_width = Q_HEADS * HEAD
    qkv_width = query_width + 2 * key_width
    attn_width = qkv_width + model_width
    token_count = sequences * local_rows
    inner_width = w_gate.shape[1]
    own_spans = lax.dynamic_slice_in_dim(span_order, lax.axis_index("ctx") * 2, 2)
    holder = jnp.argsort(span_order).astype(jnp.int32)
    own_places = (
        own_spans[:, None] * span_size + jnp.arange(span_size, dtype=jnp.int32)[None, :]
    ).reshape(local_rows)
    cosine, sine_part = rope_tables(jnp.tile(own_places, sequences))

    gains = jnp.stack([norm_one, norm_two], axis=1)
    attn_shard = jnp.concatenate(
        [w_query, w_key, w_value, w_out, jnp.pad(gains, ((0, 0), (0, PAD - 2)))], axis=1
    )
    attn_every = lax.all_gather(attn_shard, "fsdp", axis=0, tiled=True)
    gate_up = gather_columns(jnp.concatenate([w_gate, w_up], axis=1))
    down_matrix = gather_rows(w_down)
    qkv_matrix = attn_every[:, :qkv_width]
    out_matrix = attn_every[:, qkv_width:attn_width]
    gain_one = attn_every[:, attn_width].astype(jnp.float32)
    gain_two = attn_every[:, attn_width + 1].astype(jnp.float32)

    hidden_in = tokens.reshape(token_count, model_width).astype(jnp.float32)
    normed = rms_norm(hidden_in, gain_one).astype(jnp.bfloat16)
    kv_pre = product(qkv_matrix[:, query_width:], normed, "dh,nd->hn")
    keys_own = rotate(kv_pre[:key_width], cosine, sine_part).astype(jnp.bfloat16)
    kv_own = jnp.stack([keys_own, kv_pre[key_width:].astype(jnp.bfloat16)], axis=0)
    kv_every = gather_ctx(kv_own)
    query_pre = product(qkv_matrix[:, :query_width], normed, "dh,nd->hn")
    queries = (rotate(query_pre, cosine, sine_part) * 0.125).astype(jnp.bfloat16)

    attended, lse = attend(holder, own_spans, queries, kv_every, local_rows)
    middle = hidden_in + product(attended, out_matrix, "hn,hd->nd")

    normed_two = rms_norm(middle, gain_two).astype(jnp.bfloat16)
    gate_pre = mm(normed_two, gate_up[:, :inner_width])
    up_pre = mm(normed_two, gate_up[:, inner_width:])
    inner_act = swish_gate(gate_pre, up_pre).astype(jnp.bfloat16)
    output = middle + mm(inner_act, down_matrix)

    upstream_low = cotangent.reshape(token_count, model_width)
    upstream = upstream_low.astype(jnp.float32)
    grad_inner = product(upstream_low, down_matrix, "nd,fd->nf")
    _, inner_pull = jax.vjp(swish_gate, gate_pre, up_pre)
    grad_gate_pre, grad_up_pre = inner_pull(grad_inner)
    grad_gate_up_pre = jnp.concatenate(
        [grad_gate_pre.astype(jnp.bfloat16), grad_up_pre.astype(jnp.bfloat16)], axis=1
    )
    grad_normed_two = product(grad_gate_up_pre, gate_up, "nf,df->nd")
    grad_down = product(inner_act, upstream_low, "nf,nd->fd").astype(jnp.bfloat16)
    grad_gate_up = product(normed_two, grad_gate_up_pre, "nd,nf->df").astype(jnp.bfloat16)
    grad_down, grad_gate_up, grad_normed_two = lax.optimization_barrier(
        (grad_down, grad_gate_up, grad_normed_two)
    )
    quarters = column_quarters(grad_gate_up)
    shards = lax.axis_size("fsdp")
    block = quarters.shape[-1]
    grad_mlp = jnp.concatenate(
        [quarters[q].reshape(shards, -1, block) for q in range(4)]
        + [
            jnp.pad(
                grad_down.reshape(shards, -1, model_width),
                ((0, 0), (0, 0), (0, block - model_width)),
            )
        ],
        axis=1,
    )
    mlp_part = lax.psum_scatter(grad_mlp, "fsdp", scatter_dimension=0, tiled=False)

    _, second_pull = jax.vjp(rms_norm, middle, gain_two)
    grad_middle_norm, grad_gain_two = second_pull(grad_normed_two)
    grad_middle = upstream + grad_middle_norm
    middle_low = grad_middle.astype(jnp.bfloat16)
    grad_attended = product(out_matrix, middle_low, "hd,nd->hn").astype(jnp.bfloat16)

    query_grads, kv_grads = attend_back(
        holder, own_spans, queries, grad_attended, attended, lse, kv_every, local_rows
    )
    kv_grads, mlp_part = lax.optimization_barrier((kv_grads, mlp_part))
    kv_mine = scatter_ctx(kv_grads)
    grad_out = product(attended, middle_low, "hn,nd->hd")
    query_low = (rotate(query_grads, cosine, -sine_part) * 0.125).astype(jnp.bfloat16)
    key_low = rotate(kv_mine[0].astype(jnp.float32), cosine, -sine_part).astype(jnp.bfloat16)
    qkv_low = jnp.concatenate([query_low, key_low, kv_mine[1]], axis=0)
    grad_qkv = product(normed, qkv_low, "nd,hn->dh")
    grad_normed = product(qkv_low, qkv_matrix, "hn,dh->nd")
    _, first_pull = jax.vjp(rms_norm, hidden_in, gain_one)
    grad_hidden_norm, grad_gain_one = first_pull(grad_normed)
    grad_input = grad_middle + grad_hidden_norm

    grad_gains = jnp.pad(
        jnp.stack([grad_gain_one, grad_gain_two], axis=1), ((0, 0), (0, GRAD_PAD - 2))
    )
    attn_grads = jnp.concatenate([grad_qkv, grad_out, grad_gains], axis=1).astype(jnp.bfloat16)
    attn_sum = reduce_columns(attn_grads)
    mlp_sum = lax.psum(mlp_part, "ctx").astype(jnp.float32)
    rows = model_width // shards
    gate_up_sum = jnp.concatenate([mlp_sum[q * rows : (q + 1) * rows] for q in range(4)], axis=1)
    down_sum = mlp_sum[4 * rows :, :model_width]
    key_start = query_width
    value_start = query_width + key_width
    return (
        output.astype(jnp.bfloat16).reshape(tokens.shape),
        grad_input.reshape(tokens.shape),
        attn_sum[:, attn_width],
        attn_sum[:, :key_start],
        attn_sum[:, key_start:value_start],
        attn_sum[:, value_start:qkv_width],
        attn_sum[:, qkv_width:attn_width],
        attn_sum[:, attn_width + 1],
        gate_up_sum[:, :inner_width],
        gate_up_sum[:, inner_width:],
        down_sum,
    )


def solution(mesh):
    in_specs = (
        P("fsdp", "ctx", None),
        P("fsdp", "ctx", None),
        P(),
        P("fsdp"),
        P("fsdp", None),
        P("fsdp", None),
        P("fsdp", None),
        P("fsdp", None),
        P("fsdp"),
        P("fsdp", None),
        P("fsdp", None),
        P("fsdp", None),
    )
    out_specs = (
        P("fsdp", "ctx", None),
        P("fsdp", "ctx", None),
        P("fsdp"),
        P("fsdp", None),
        P("fsdp", None),
        P("fsdp", None),
        P("fsdp", None),
        P("fsdp"),
        P("fsdp", None),
        P("fsdp", None),
        P("fsdp", None),
    )
    return jax.shard_map(body, mesh=mesh, in_specs=in_specs, out_specs=out_specs, check_vma=False)
```
